32 devices in a mesh: clip: 4 (over z), frame: 2 (over x), mp: 4 (over y, core).
Axes of the slice: x: 2, y: 2, z: 4, core: 2. Of those that a mesh axis runs over, the one named last changes fastest.
Arguments:
- query_spatial: bfloat16 [4, 2, 2, 40, 2560], P('clip', 'frame', None, None, 'mp'), may hold values from -24 to 24
- key_spatial: bfloat16 [4, 2, 2, 40, 2560], P('clip', 'frame', None, None, 'mp'), may hold values from -24 to 24
- value_spatial: bfloat16 [4, 2, 2, 40, 2560], P('clip', 'frame', None, None, 'mp'), may hold values from -10 to 10
- gains: float32 [3, 2560], P(None, 'mp'), may hold values from 0.5 to 2.5
- warp_lists: int32 [4, 2, 2], P('clip', 'frame'), may hold values from 0 to 1
- cotangent: bfloat16 [4, 2, 2, 40, 2560], P('clip', None, 'frame', None, 'mp'), may hold values from -3 to 3
Outputs:
- temporal_out: bfloat16 [4, 2, 2, 40, 2560], P('clip', None, 'frame', None, 'mp')
- grad_query: bfloat16 [4, 2, 2, 40, 2560], P('clip', 'frame', None, None, 'mp')
- grad_key: bfloat16 [4, 2, 2, 40, 2560], P('clip', 'frame', None, None, 'mp')
- grad_value: bfloat16 [4, 2, 2, 40, 2560], P('clip', 'frame', None, None, 'mp')
- grad_gains: float32 [3, 2560], P(None, 'mp')
The draws below stay inside these ranges and needn't reach their ends.
All inputs are finite; a program needn't handle non-finite values.
Results may differ from the reference program's by a relative error of at most 0.035.
Values may be sent and summed in bfloat16 or wider, within the bound.
A program may use at most 128 MiB of HBM per device.

```python
import math
import jax
import jax.numpy as jnp
from jax import lax

HEADS = 20
HD = 128
TT = 40
WIDTH = 2560
CLIPS = 4
FRAMES = 2
TILES = 2


def pair_draw(key):
    key_first, key_second = jax.random.split(jax.random.fold_in(key, 17), 2)
    shape = (CLIPS, FRAMES, TILES, TT, HEADS * HD)
    query_all = 1.6 * jax.random.normal(key_first, shape, jnp.float32)
    key_all = 1.6 * jax.random.normal(key_second, shape, jnp.float32)
    return (jnp.clip(query_all, -24.0, 24.0), jnp.clip(key_all, -24.0, 24.0))


def draw_query_spatial(key, part):
    return pair_draw(key)[0].astype(jnp.bfloat16)


def draw_key_spatial(key, part):
    return pair_draw(key)[1].astype(jnp.bfloat16)


def draw_value_spatial(key, part):
    shape = (CLIPS, FRAMES, TILES, TT, HEADS * HD)
    head_of = (jnp.arange(HEADS * HD) // HD).astype(jnp.float32)
    spread = 0.4 * 3.0 ** (head_of / max(HEADS - 1, 1))
    inner_key = jax.random.fold_in(key, 23)
    values = jax.random.normal(inner_key, shape, jnp.float32)
    return jnp.clip(values * spread, -10.0, 10.0).astype(jnp.bfloat16)


def draw_gains(key, part):
    inner_key = jax.random.fold_in(key, 29)
    upper = jnp.log(2.0)
    logs = jax.random.uniform(inner_key, (3, HEADS * HD), jnp.float32, jnp.log(0.5), upper)
    return jnp.exp(logs)


def with_ends(entries, key, low, largest):
    longest = entries.shape.index(max(entries.shape))
    spots = []
    for shift in (0, 1):
        where = [jax.random.randint(jax.random.fold_in(key, axis), (), 0, length) for axis, length in enumerate(entries.shape)]
        where[longest] = (where[longest] + shift) % entries.shape[longest]
        spots.append(tuple(where))
    return entries.at[spots[0]].set(low).at[spots[1]].set(largest)


def block_scale(key, dims, cuts, least, high):
    gain = 1.0
    for axis_at, blocks in cuts:
        heights = jax.random.uniform(jax.random.fold_in(jax.random.fold_in(key, 6), axis_at), (blocks,), jnp.float32, least / len(cuts), high / len(cuts))
        gain = gain * jnp.repeat(jnp.exp(heights), dims[axis_at] // blocks).reshape((-1,) + (1,) * (len(dims) - 1 - axis_at))
    return gain


def gaussian(key, dims, deviation, reach, cuts=(), kind=jnp.bfloat16):
    level = block_scale(key, dims, cuts, -0.22, 0.18) if cuts else 1.0
    values = jax.random.normal(key, dims, jnp.float32) * deviation * level
    return jnp.minimum(jnp.maximum(values, -reach), reach).astype(kind)


def setup_inputs(seed: int = 0) -> dict:
    keys = jax.random.split(jax.random.key(seed), 7)
    query_spatial = draw_query_spatial(jax.random.fold_in(keys[6], 71), 0)
    key_spatial = draw_key_spatial(jax.random.fold_in(keys[6], 71), 0)
    value_spatial = draw_value_spatial(jax.random.fold_in(keys[6], 71), 0)
    gains = draw_gains(jax.random.fold_in(keys[6], 71), 0)
    warp_lists = with_ends(jax.random.randint(keys[4], (CLIPS, FRAMES, TILES), 0, TILES), jax.random.fold_in(keys[4], 1), 0, TILES - 1).astype(jnp.int32)
    cotangent = gaussian(keys[5], (CLIPS, FRAMES, TILES, TT, WIDTH), 0.5, 3.0, ((0, 4), (2, 2), (4, 4)))
    return dict(query_spatial=query_spatial, key_spatial=key_spatial, value_spatial=value_spatial, gains=gains, warp_lists=warp_lists, cotangent=cotangent)


epsilon = 1e-06

def attend_weights(queries, key_rows, visible):
    head_dim = queries.shape[-1]
    scores = jnp.einsum('qhd,khd->hqk', queries.astype(jnp.float32), key_rows.astype(jnp.float32)) / math.sqrt(head_dim)
    scores = jnp.where(visible[None], scores, -1e+30)
    top = lax.optimization_barrier(jnp.max(scores, axis=-1, keepdims=True))
    expon = jnp.exp(scores - top)
    return expon / lax.optimization_barrier(jnp.sum(expon, axis=-1, keepdims=True))

def attend_forward(queries, key_rows, value_rows, visible):
    weights = attend_weights(queries, key_rows, visible)
    rounded = weights.astype(jnp.bfloat16)
    output = jnp.einsum('hqk,khd->qhd', rounded.astype(jnp.float32), value_rows.astype(jnp.float32))
    return output.astype(jnp.bfloat16)

def attend_backward(queries, key_rows, value_rows, upstream, visible):
    head_dim = queries.shape[-1]
    weights = attend_weights(queries, key_rows, visible)
    rounded = weights.astype(jnp.bfloat16)
    grad_weights = jnp.einsum('qhd,khd->hqk', upstream.astype(jnp.float32), value_rows.astype(jnp.float32))
    inner = lax.optimization_barrier(jnp.sum(weights * grad_weights, axis=-1, keepdims=True))
    grad_scores = (weights * (grad_weights - inner) / math.sqrt(head_dim)).astype(jnp.bfloat16)
    grad_queries = jnp.einsum('hqk,khd->qhd', grad_scores.astype(jnp.float32), key_rows.astype(jnp.float32))
    grad_keys = jnp.einsum('hqk,qhd->khd', grad_scores.astype(jnp.float32), queries.astype(jnp.float32))
    grad_values = jnp.einsum('hqk,qhd->khd', rounded.astype(jnp.float32), upstream.astype(jnp.float32))
    return (grad_queries, grad_keys, grad_values)

def reference(query_spatial, key_spatial, value_spatial, gains, warp_lists, cotangent):
    gain_query = gains[0]
    gain_key = gains[1]
    gain_value = gains[2]

    def one_clip(inputs):
        query_clip, key_clip, value_clip, warp_clip, cotan_clip = inputs
        frames, tiles, tile_tok, width = query_clip.shape
        heads = width // HD
        count = tiles * tile_tok

        def to_heads(array):
            return array.reshape(frames, count, heads, HD)
        all_visible = jnp.ones((count, count), bool)
        spatial = lax.map(lambda trio: attend_forward(trio[0], trio[1], trio[2], all_visible), (to_heads(query_clip), to_heads(key_clip), to_heads(value_clip)))
        spatial = spatial.reshape(frames, tiles, tile_tok, width)
        spatial_f = spatial.astype(jnp.float32)
        inverse = lax.rsqrt(lax.optimization_barrier(jnp.mean(spatial_f * spatial_f, axis=-1, keepdims=True)) + epsilon)
        normed = (spatial_f * inverse).astype(jnp.bfloat16)
        warped = jax.vmap(lambda field, rows: field[rows])(normed, warp_clip)
        tile_query = (normed.astype(jnp.float32) * gain_query).astype(jnp.bfloat16)
        tile_key = (warped.astype(jnp.float32) * gain_key).astype(jnp.bfloat16)
        tile_value = (warped.astype(jnp.float32) * gain_value).astype(jnp.bfloat16)

        def tile_major(array):
            return jnp.transpose(array, (1, 0, 2, 3)).reshape(tiles, frames * tile_tok, heads, HD)

        def frame_major(array):
            return jnp.transpose(array.reshape(tiles, frames, tile_tok, width), (1, 0, 2, 3))
        frame_of = jnp.arange(frames * tile_tok) // tile_tok
        causal = frame_of[:, None] >= frame_of[None, :]
        temporal = lax.map(lambda trio: attend_forward(trio[0], trio[1], trio[2], causal), (tile_major(tile_query), tile_major(tile_key), tile_major(tile_value)))
        grads = lax.map(lambda quad: attend_backward(quad[0], quad[1], quad[2], quad[3], causal), (tile_major(tile_query), tile_major(tile_key), tile_major(tile_value), tile_major(cotan_clip)))
        rounded = lax.optimization_barrier((grads[0].astype(jnp.bfloat16), grads[1].astype(jnp.bfloat16), grads[2].astype(jnp.bfloat16)))
        grad_tq = frame_major(rounded[0]).astype(jnp.float32)
        grad_tk = frame_major(rounded[1]).astype(jnp.float32)
        grad_tv = frame_major(rounded[2]).astype(jnp.float32)
        gain_terms = jnp.stack([lax.optimization_barrier(jnp.sum(grad_tq * normed.astype(jnp.float32), axis=(0, 1, 2))), lax.optimization_barrier(jnp.sum(grad_tk * warped.astype(jnp.float32), axis=(0, 1, 2))), lax.optimization_barrier(jnp.sum(grad_tv * warped.astype(jnp.float32), axis=(0, 1, 2)))])
        direct = grad_tq * gain_query
        moved = grad_tk * gain_key + grad_tv * gain_value
        onehot = (warp_clip[:, :, None] == jnp.arange(tiles)[None, None, :]).astype(jnp.float32)
        grad_normed = direct + jnp.einsum('tjs,tjaf->tsaf', onehot, moved, precision=lax.Precision.HIGHEST)
        inner = lax.optimization_barrier(jnp.mean(grad_normed * spatial_f, axis=-1, keepdims=True))
        grad_spatial = (inverse * grad_normed - spatial_f * inverse ** 3 * inner).astype(jnp.bfloat16)
        back = lax.map(lambda quad: attend_backward(quad[0], quad[1], quad[2], quad[3], all_visible), (to_heads(query_clip), to_heads(key_clip), to_heads(value_clip), to_heads(grad_spatial)))
        shape = (frames, tiles, tile_tok, width)
        return (frame_major(temporal), back[0].reshape(shape).astype(jnp.bfloat16), back[1].reshape(shape).astype(jnp.bfloat16), back[2].reshape(shape).astype(jnp.bfloat16), gain_terms)
    results = lax.map(one_clip, (query_spatial, key_spatial, value_spatial, warp_lists, cotangent))
    return (results[0], results[1], results[2], results[3], lax.optimization_barrier(jnp.sum(results[4], axis=0)))
```

```python
import functools
import math

import jax
import jax.numpy as jnp
from jax import lax
from jax.experimental import pallas as pl
from jax.experimental.pallas import tpu as pltpu
from jax.sharding import PartitionSpec as P

HD = 128
MESH = pl.DeviceIdType.MESH
epsilon = 1e-06
F32 = jnp.float32
BF16 = jnp.bfloat16


def pad8(n):
    return (n + 7) // 8 * 8


def dot_nt(a, b):
    return lax.dot_general(a, b, (((1,), (1,)), ((), ())), preferred_element_type=F32)


def dot_nn(a, b):
    return lax.dot_general(a, b, (((1,), (0,)), ((), ())), preferred_element_type=F32)


def dot_tn(a, b):
    return lax.dot_general(a, b, (((0,), (0,)), ((), ())), preferred_element_type=F32)


def softmax(scores):
    top = jnp.max(scores, axis=-1, keepdims=True)
    expon = jnp.exp(scores - top)
    return expon / jnp.sum(expon, axis=-1, keepdims=True)


def kernel(
    dims,
    q_ref,
    k_ref,
    v_ref,
    gains_ref,
    warp_ref,
    cot_ref,
    tout_ref,
    gq_ref,
    gk_ref,
    gv_ref,
    gg_ref,
    p_sc,
    sp_sc,
    table_sc,
    a_send,
    a_recv,
    sq_send,
    sq_recv,
    b_send,
    b_recv,
    in_send,
    in_recv,
    g_send,
    g_recv,
    a_ss,
    a_rs,
    sq_ss,
    sq_rs,
    b_ss,
    b_rs,
    in_ss,
    in_rs,
    g_ss,
    g_rs,
):
    clips, frames, mps, tiles, tt, heads = dims
    total_width = float(heads * HD * mps)
    scale = 1.0 / math.sqrt(HD)
    c = lax.axis_index("clip")
    f = lax.axis_index("frame")
    m = lax.axis_index("mp")

    def at(index, step, size):
        return lax.rem(index + step, size) if step else index

    group = [(df, dm) for df in range(frames) for dm in range(mps) if (df, dm) != (0, 0)]
    wide = [(dc, df) for dc in range(clips) for df in range(frames) if (dc, df) != (0, 0)]

    def in_group(df, dm):
        return {"frame": at(f, df, frames), "mp": at(m, dm, mps)}

    def in_wide(dc, df):
        return {"clip": at(c, dc, clips), "frame": at(f, df, frames)}

    barrier = pltpu.get_barrier_semaphore()
    peers = [in_group(*step) for step in group]
    peers += [in_wide(dc, df) for dc, df in wide if dc]
    for peer in peers:
        pl.semaphore_signal(barrier, inc=1, device_id=peer, device_id_type=MESH)

    def head_cols(h):
        if isinstance(h, int):
            return slice(h * HD, (h + 1) * HD)
        return pl.ds(pl.multiple_of(h * HD, HD), HD)

    def each_head(fn, carry):
        if tiles * tt <= 128:
            for h in range(heads):
                carry = fn(h, carry)
            return carry
        return lax.fori_loop(0, heads, fn, carry)

    def send(src, dst, send_sem, recv_sem, peer):
        copy = pltpu.make_async_remote_copy(
            src_ref=src,
            dst_ref=dst,
            send_sem=send_sem,
            recv_sem=recv_sem,
            device_id=peer,
            device_id_type=MESH,
        )
        copy.start()
        return copy

    diagonal = lax.broadcasted_iota(jnp.int32, (tt, HD), 0) == lax.broadcasted_iota(
        jnp.int32, (tt, HD), 1
    )

    def to_row(column):
        return jnp.sum(jnp.where(diagonal, column, 0.0), axis=0, keepdims=True)

    def to_column(row):
        return jnp.sum(jnp.where(diagonal, row, 0.0), axis=1, keepdims=True)

    def spatial_head(h, squares):
        cols = head_cols(h)
        weights = softmax(dot_nt(q_ref[:, cols], k_ref[:, cols]) * scale)
        p_sc[h] = weights
        out = dot_nn(weights.astype(BF16), v_ref[:, cols]).astype(BF16).astype(F32)
        sp_sc[:, cols] = out
        return squares + out * out

    squares = each_head(spatial_head, jnp.zeros((tiles * tt, HD), F32))
    square_sum = jnp.sum(squares, axis=1, keepdims=True)
    for s in range(tiles):
        table_sc[pl.ds(s, 1), :] = to_row(square_sum[s * tt : (s + 1) * tt])

    def reads(j, s):
        return jnp.where(jnp.full((1, HD), warp_ref[j], jnp.int32) == s, 1.0, 0.0)

    def tile_pair(ref, j):
        picks = [reads(j, s) for s in range(tiles)]

        def one_head(h, carry):
            cols = head_cols(h)
            own = sp_sc[pl.ds(pl.multiple_of(j * tt, 8), tt), cols]
            source = picks[0] * sp_sc[0:tt, cols]
            for s in range(1, tiles):
                source = source + picks[s] * sp_sc[s * tt : (s + 1) * tt, cols]
            ref[:, cols] = jnp.concatenate([own, source], axis=0).astype(BF16)
            return carry

        each_head(one_head, 0)

    def square_rows(ref, j):
        source = reads(j, 0) * table_sc[0:1, :]
        for s in range(1, tiles):
            source = source + reads(j, s) * table_sc[s : s + 1, :]
        ref[0:1, :] = table_sc[pl.ds(j, 1), :]
        ref[1:2, :] = source
        ref[2 : 2 + tiles, :] = table_sc[0:tiles, :]

    pl.semaphore_wait(barrier, len(peers))

    flying = []
    for df in range(1, frames):
        j = at(f, df, frames)
        tile_pair(a_send.at[df], j)
        flying.append(send(a_send.at[df], a_recv.at[f], a_ss.at[df], a_rs.at[df], {"frame": j}))
    for df in range(frames):
        square_rows(sq_send.at[df], at(f, df, frames))
    for df, dm in group:
        flying.append(
            send(
                sq_send.at[df],
                sq_recv.at[f, m],
                sq_ss.at[df, dm],
                sq_rs.at[df, dm],
                in_group(df, dm),
            )
        )
    tile_pair(a_recv.at[f], f)
    sq_recv[f, m] = sq_send[0]
    for copy in flying:
        copy.wait()

    inverse_rows = []
    for t in range(frames):
        total = sq_recv[t, 0]
        for other in range(1, mps):
            total = total + sq_recv[t, other]
        inverse_rows.append(lax.rsqrt(total / total_width + epsilon))
    inverse_own = jnp.concatenate([to_column(rows[0:1]) for rows in inverse_rows], axis=0)
    inverse_source = jnp.concatenate([to_column(rows[1:2]) for rows in inverse_rows], axis=0)
    count = frames * tt
    frame_q = lax.broadcasted_iota(jnp.int32, (count, count), 0) // tt
    frame_k = lax.broadcasted_iota(jnp.int32, (count, count), 1) // tt
    causal = frame_q >= frame_k

    def temporal_head(h, carry):
        dot_own, dot_source = carry
        cols = head_cols(h)
        blocks = [a_recv[t, :, cols].astype(F32) for t in range(frames)]
        own = jnp.concatenate([block[:tt] for block in blocks], axis=0)
        source = jnp.concatenate([block[tt:] for block in blocks], axis=0)
        normed = (own * inverse_own).astype(BF16).astype(F32)
        warped = (source * inverse_source).astype(BF16).astype(F32)
        gain_q = gains_ref[0:1, cols]
        gain_k = gains_ref[1:2, cols]
        gain_v = gains_ref[2:3, cols]
        tq = (normed * gain_q).astype(BF16)
        tk = (warped * gain_k).astype(BF16)
        tv = (warped * gain_v).astype(BF16)
        weights = softmax(jnp.where(causal, dot_nt(tq, tk) * scale, -1e30))
        rounded = weights.astype(BF16)
        tout_ref[:, cols] = dot_nn(rounded, tv).astype(BF16)
        upstream = cot_ref[:, cols]
        grad_weights = dot_nt(upstream, tv)
        inner = jnp.sum(weights * grad_weights, axis=-1, keepdims=True)
        grad_scores = (weights * (grad_weights - inner) * scale).astype(BF16)
        dq = dot_nn(grad_scores, tk).astype(BF16).astype(F32)
        dk = dot_tn(grad_scores, tq).astype(BF16).astype(F32)
        dv = dot_tn(rounded, upstream).astype(BF16).astype(F32)
        direct = (dq * gain_q).astype(BF16).astype(F32)
        moved = (dk * gain_k + dv * gain_v).astype(BF16).astype(F32)
        for t in range(frames):
            rows = slice(t * tt, (t + 1) * tt)
            b_send[t, :, cols] = jnp.concatenate([direct[rows], moved[rows]], axis=0).astype(BF16)
        g_send[pl.ds(h, 1), :] = jnp.sum(dq * normed, axis=0, keepdims=True)
        g_send[pl.ds(heads + h, 1), :] = jnp.sum(dk * warped, axis=0, keepdims=True)
        g_send[pl.ds(2 * heads + h, 1), :] = jnp.sum(dv * warped, axis=0, keepdims=True)
        return dot_own + direct * own, dot_source + moved * source

    zero = jnp.zeros((count, HD), F32)
    dot_own, dot_source = each_head(temporal_head, (zero, zero))

    flying = []
    for df in range(1, frames):
        t = at(f, df, frames)
        flying.append(send(b_send.at[t], b_recv.at[f], b_ss.at[df], b_rs.at[df], {"frame": t}))
    dot_own = jnp.sum(dot_own, axis=1, keepdims=True)
    dot_source = jnp.sum(dot_source, axis=1, keepdims=True)
    for t in range(frames):
        rows = slice(t * tt, (t + 1) * tt)
        in_send[t, 0:1, :] = to_row(dot_own[rows])
        in_send[t, 1:2, :] = to_row(dot_source[rows])
    for df, dm in group:
        flying.append(
            send(
                in_send.at[at(f, df, frames)],
                in_recv.at[f, m],
                in_ss.at[df, dm],
                in_rs.at[df, dm],
                in_group(df, dm),
            )
        )
    sums = []
    for dc, df in wide:
        sums.append(
            send(g_send, g_recv.at[c, f], g_ss.at[dc, df], g_rs.at[dc, df], in_wide(dc, df))
        )
    b_recv[f] = b_send[f]
    in_recv[f, m] = in_send[f]
    g_recv[c, f] = g_send[...]
    for copy in flying:
        copy.wait()

    total = sq_recv[f, 0]
    for other in range(1, mps):
        total = total + sq_recv[f, other]
    inverse_table = lax.rsqrt(total / total_width + epsilon)
    inner_rows = []
    for j in range(tiles):
        rows = in_recv[j, 0]
        for other in range(1, mps):
            rows = rows + in_recv[j, other]
        inner_rows.append(rows)
    factors = []
    for s in range(tiles):
        row = inner_rows[s][0:1]
        for j in range(tiles):
            row = row + reads(j, s) * inner_rows[j][1:2]
        inverse = to_column(inverse_table[2 + s : 3 + s])
        inner = to_column(row)
        factors.append((inverse, inverse * inverse * inverse * (inner / total_width)))

    def backward_head(h, carry):
        cols = head_cols(h)
        blocks = [b_recv[j, :, cols].astype(F32) for j in range(tiles)]
        parts = []
        for s in range(tiles):
            grad = blocks[s][:tt]
            for j in range(tiles):
                grad = grad + reads(j, s) * blocks[j][tt:]
            inverse, factor = factors[s]
            parts.append(inverse * grad - sp_sc[s * tt : (s + 1) * tt, cols] * factor)
        upstream = jnp.concatenate(parts, axis=0).astype(BF16)
        weights = p_sc[h]
        grad_weights = dot_nt(upstream, v_ref[:, cols])
        inner = jnp.sum(weights * grad_weights, axis=-1, keepdims=True)
        grad_scores = (weights * (grad_weights - inner) * scale).astype(BF16)
        gq_ref[:, cols] = dot_nn(grad_scores, k_ref[:, cols]).astype(BF16)
        gk_ref[:, cols] = dot_tn(grad_scores, q_ref[:, cols]).astype(BF16)
        gv_ref[:, cols] = dot_tn(weights.astype(BF16), upstream).astype(BF16)
        return carry

    each_head(backward_head, 0)

    for copy in sums:
        copy.wait()
    total = None
    for other in range(clips):
        for t in range(frames):
            total = g_recv[other, t] if total is None else total + g_recv[other, t]
    for g in range(3):
        for h in range(heads):
            row = g * heads + h
            gg_ref[g : g + 1, h * HD : (h + 1) * HD] = total[row : row + 1]


def body(sizes, query, key, value, gains, warp_lists, cotangent):
    clips, frames, mps = sizes
    tiles, tt, width = query.shape[2:]
    heads = width // HD
    count = tiles * tt
    dims = (clips, frames, mps, tiles, tt, heads)
    vmem = pl.BlockSpec(memory_space=pltpu.VMEM)
    table = pad8(tiles + 2)
    gain_rows = pad8(3 * heads)
    dma = pltpu.SemaphoreType.DMA
    outs = pl.pallas_call(
        functools.partial(kernel, dims),
        out_shape=(
            jax.ShapeDtypeStruct((frames * tt, width), BF16),
            jax.ShapeDtypeStruct((count, width), BF16),
            jax.ShapeDtypeStruct((count, width), BF16),
            jax.ShapeDtypeStruct((count, width), BF16),
            jax.ShapeDtypeStruct((3, width), F32),
        ),
        in_specs=[vmem, vmem, vmem, vmem, pl.BlockSpec(memory_space=pltpu.SMEM), vmem],
        out_specs=(vmem,) * 5,
        scratch_shapes=[
            pltpu.VMEM((heads, count, count), F32),
            pltpu.VMEM((count, width), F32),
            pltpu.VMEM((pad8(tiles), HD), F32),
            pltpu.VMEM((frames, 2 * tt, width), BF16),
            pltpu.VMEM((frames, 2 * tt, width), BF16),
            pltpu.VMEM((frames, table, HD), F32),
            pltpu.VMEM((frames, mps, table, HD), F32),
            pltpu.VMEM((frames, 2 * tt, width), BF16),
            pltpu.VMEM((frames, 2 * tt, width), BF16),
            pltpu.VMEM((frames, 8, HD), F32),
            pltpu.VMEM((frames, mps, 8, HD), F32),
            pltpu.VMEM((gain_rows, HD), F32),
            pltpu.VMEM((clips, frames, gain_rows, HD), F32),
            dma((frames,)),
            dma((frames,)),
            dma((frames, mps)),
            dma((frames, mps)),
            dma((frames,)),
            dma((frames,)),
            dma((frames, mps)),
            dma((frames, mps)),
            dma((clips, frames)),
            dma((clips, frames)),
        ],
        compiler_params=pltpu.CompilerParams(
            collective_id=0, has_side_effects=True, vmem_limit_bytes=56 * 2**20
        ),
    )(
        query.reshape(count, width),
        key.reshape(count, width),
        value.reshape(count, width),
        gains,
        warp_lists.reshape(tiles),
        cotangent.reshape(frames * tt, width),
    )
    temporal, back_q, back_k, back_v, grad_gains = outs
    return (
        temporal.reshape(cotangent.shape),
        back_q.reshape(query.shape),
        back_k.reshape(query.shape),
        back_v.reshape(query.shape),
        grad_gains,
    )


def solution(mesh):
    sizes = (mesh.shape["clip"], mesh.shape["frame"], mesh.shape["mp"])
    return jax.shard_map(
        functools.partial(body, sizes),
        mesh=mesh,
        in_specs=(
            P("clip", "frame", None, None, "mp"),
            P("clip", "frame", None, None, "mp"),
            P("clip", "frame", None, None, "mp"),
            P(None, "mp"),
            P("clip", "frame", None),
            P("clip", None, "frame", None, "mp"),
        ),
        out_specs=(
            P("clip", None, "frame", None, "mp"),
            P("clip", "frame", None, None, "mp"),
            P("clip", "frame", None, None, "mp"),
            P("clip", "frame", None, None, "mp"),
            P(None, "mp"),
        ),
        check_vma=False,
    )
```

```python
import functools
import math

import jax
import jax.numpy as jnp
from jax import lax
from jax.experimental import pallas as pl
from jax.experimental.pallas import tpu as pltpu
from jax.sharding import PartitionSpec as P

HD = 128
MESH = pl.DeviceIdType.MESH
epsilon = 1e-06
F32 = jnp.float32
BF16 = jnp.bfloat16


def pad8(n):
    return (n + 7) // 8 * 8


def dot_nt(a, b):
    return lax.dot_general(a, b, (((1,), (1,)), ((), ())), preferred_element_type=F32)


def dot_nn(a, b):
    return lax.dot_general(a, b, (((1,), (0,)), ((), ())), preferred_element_type=F32)


def dot_tn(a, b):
    return lax.dot_general(a, b, (((0,), (0,)), ((), ())), preferred_element_type=F32)


def softmax(scores):
    top = jnp.max(scores, axis=-1, keepdims=True)
    expon = jnp.exp(scores - top)
    return expon / jnp.sum(expon, axis=-1, keepdims=True)


def kernel(
    dims,
    q_ref,
    k_ref,
    v_ref,
    gains_ref,
    warp_ref,
    cot_ref,
    tout_ref,
    gq_ref,
    gk_ref,
    gv_ref,
    gg_ref,
    p_sc,
    sp_sc,
    table_sc,
    a_send,
    a_recv,
    sq_send,
    sq_recv,
    b_send,
    b_recv,
    in_send,
    in_recv,
    g_send,
    g_recv,
    a_ss,
    a_rs,
    sq_ss,
    sq_rs,
    b_ss,
    b_rs,
    in_ss,
    in_rs,
    g_ss,
    g_rs,
):
    clips, frames, mps, tiles, tt, heads = dims
    total_width = float(heads * HD * mps)
    scale = 1.0 / math.sqrt(HD)
    c = lax.axis_index("clip")
    f = lax.axis_index("frame")
    m = lax.axis_index("mp")

    def at(index, step, size):
        return lax.rem(index + step, size) if step else index

    group = [(df, dm) for df in range(frames) for dm in range(mps) if (df, dm) != (0, 0)]
    wide = [(dc, df) for dc in range(clips) for df in range(frames) if (dc, df) != (0, 0)]

    def in_group(df, dm):
        return {"frame": at(f, df, frames), "mp": at(m, dm, mps)}

    def in_wide(dc, df):
        return {"clip": at(c, dc, clips), "frame": at(f, df, frames)}

    barrier = pltpu.get_barrier_semaphore()
    peers = [in_group(*step) for step in group]
    peers += [in_wide(dc, df) for dc, df in wide if dc]
    for peer in peers:
        pl.semaphore_signal(barrier, inc=1, device_id=peer, device_id_type=MESH)

    def head_cols(h):
        if isinstance(h, int):
            return slice(h * HD, (h + 1) * HD)
        return pl.ds(pl.multiple_of(h * HD, HD), HD)

    def each_head(fn, carry):
        if tiles * tt <= 128:
            for h in range(heads):
                carry = fn(h, carry)
            return carry
        return lax.fori_loop(0, heads, fn, carry)

    def send(src, dst, send_sem, recv_sem, peer):
        copy = pltpu.make_async_remote_copy(
            src_ref=src,
            dst_ref=dst,
            send_sem=send_sem,
            recv_sem=recv_sem,
            device_id=peer,
            device_id_type=MESH,
        )
        copy.start()
        return copy

    diagonal = lax.broadcasted_iota(jnp.int32, (tt, HD), 0) == lax.broadcasted_iota(
        jnp.int32, (tt, HD), 1
    )

    def to_row(column):
        return jnp.sum(jnp.where(diagonal, column, 0.0), axis=0, keepdims=True)

    def to_column(row):
        return jnp.sum(jnp.where(diagonal, row, 0.0), axis=1, keepdims=True)

    def spatial_head(h, squares):
        cols = head_cols(h)
        weights = softmax(dot_nt(q_ref[:, cols], k_ref[:, cols]) * scale)
        p_sc[h] = weights
        out = dot_nn(weights.astype(BF16), v_ref[:, cols]).astype(BF16).astype(F32)
        sp_sc[:, cols] = out
        return squares + out * out

    squares = each_head(spatial_head, jnp.zeros((tiles * tt, HD), F32))
    square_sum = jnp.sum(squares, axis=1, keepdims=True)
    for s in range(tiles):
        table_sc[pl.ds(s, 1), :] = to_row(square_sum[s * tt : (s + 1) * tt])

    def reads(j, s):
        return jnp.where(jnp.full((1, HD), warp_ref[j], jnp.int32) == s, 1.0, 0.0)

    def tile_pair(ref, j):
        picks = [reads(j, s) for s in range(tiles)]

        def one_head(h, carry):
            cols = head_cols(h)
            own = sp_sc[pl.ds(pl.multiple_of(j * tt, 8), tt), cols]
            source = picks[0] * sp_sc[0:tt, cols]
            for s in range(1, tiles):
                source = source + picks[s] * sp_sc[s * tt : (s + 1) * tt, cols]
            ref[:, cols] = jnp.concatenate([own, source], axis=0).astype(BF16)
            return carry

        each_head(one_head, 0)

    def square_rows(ref, j):
        source = reads(j, 0) * table_sc[0:1, :]
        for s in range(1, tiles):
            source = source + reads(j, s) * table_sc[s : s + 1, :]
        ref[0:1, :] = table_sc[pl.ds(j, 1), :]
        ref[1:2, :] = source
        ref[2 : 2 + tiles, :] = table_sc[0:tiles, :]

    pl.semaphore_wait(barrier, len(peers))

    flying = []
    for df in range(1, frames):
        j = at(f, df, frames)
        tile_pair(a_send.at[df], j)
        flying.append(send(a_send.at[df], a_recv.at[f], a_ss.at[df], a_rs.at[df], {"frame": j}))
    for df in range(frames):
        square_rows(sq_send.at[df], at(f, df, frames))
    for df, dm in group:
        flying.append(
            send(
                sq_send.at[df],
                sq_recv.at[f, m],
                sq_ss.at[df, dm],
                sq_rs.at[df, dm],
                in_group(df, dm),
            )
        )
    tile_pair(a_recv.at[f], f)
    sq_recv[f, m] = sq_send[0]
    for copy in flying:
        copy.wait()

    inverse_rows = []
    for t in range(frames):
        total = sq_recv[t, 0]
        for other in range(1, mps):
            total = total + sq_recv[t, other]
        inverse_rows.append(lax.rsqrt(total / total_width + epsilon))
    inverse_own = jnp.concatenate([to_column(rows[0:1]) for rows in inverse_rows], axis=0)
    inverse_source = jnp.concatenate([to_column(rows[1:2]) for rows in inverse_rows], axis=0)
    count = frames * tt
    frame_q = lax.broadcasted_iota(jnp.int32, (count, count), 0) // tt
    frame_k = lax.broadcasted_iota(jnp.int32, (count, count), 1) // tt
    causal = frame_q >= frame_k

    def temporal_head(h, carry):
        dot_own, dot_source = carry
        cols = head_cols(h)
        blocks = [a_recv[t, :, cols].astype(F32) for t in range(frames)]
        own = jnp.concatenate([block[:tt] for block in blocks], axis=0)
        source = jnp.concatenate([block[tt:] for block in blocks], axis=0)
        normed = (own * inverse_own).astype(BF16).astype(F32)
        warped = (source * inverse_source).astype(BF16).astype(F32)
        gain_q = gains_ref[0:1, cols]
        gain_k = gains_ref[1:2, cols]
        gain_v = gains_ref[2:3, cols]
        tq = (normed * gain_q).astype(BF16)
        tk = (warped * gain_k).astype(BF16)
        tv = (warped * gain_v).astype(BF16)
        weights = softmax(jnp.where(causal, dot_nt(tq, tk) * scale, -1e30))
        rounded = weights.astype(BF16)
        tout_ref[:, cols] = dot_nn(rounded, tv).astype(BF16)
        upstream = cot_ref[:, cols]
        grad_weights = dot_nt(upstream, tv)
        inner = jnp.sum(weights * grad_weights, axis=-1, keepdims=True)
        grad_scores = (weights * (grad_weights - inner) * scale).astype(BF16)
        dq = dot_nn(grad_scores, tk).astype(BF16).astype(F32)
        dk = dot_tn(grad_scores, tq).astype(BF16).astype(F32)
        dv = dot_tn(rounded, upstream).astype(BF16).astype(F32)
        direct = (dq * gain_q).astype(BF16).astype(F32)
        moved = (dk * gain_k + dv * gain_v).astype(BF16).astype(F32)
        for t in range(frames):
            rows = slice(t * tt, (t + 1) * tt)
            b_send[t, :, cols] = jnp.concatenate([direct[rows], moved[rows]], axis=0).astype(BF16)
        g_send[pl.ds(h, 1), :] = jnp.sum(dq * normed, axis=0, keepdims=True)
        g_send[pl.ds(heads + h, 1), :] = jnp.sum(dk * warped, axis=0, keepdims=True)
        g_send[pl.ds(2 * heads + h, 1), :] = jnp.sum(dv * warped, axis=0, keepdims=True)
        return dot_own + direct * own, dot_source + moved * source

    zero = jnp.zeros((count, HD), F32)
    dot_own, dot_source = each_head(temporal_head, (zero, zero))

    flying = []
    for df in range(1, frames):
        t = at(f, df, frames)
        flying.append(send(b_send.at[t], b_recv.at[f], b_ss.at[df], b_rs.at[df], {"frame": t}))
    dot_own = jnp.sum(dot_own, axis=1, keepdims=True)
    dot_source = jnp.sum(dot_source, axis=1, keepdims=True)
    for t in range(frames):
        rows = slice(t * tt, (t + 1) * tt)
        in_send[t, 0:1, :] = to_row(dot_own[rows])
        in_send[t, 1:2, :] = to_row(dot_source[rows])
    for df, dm in group:
        flying.append(
            send(
                in_send.at[at(f, df, frames)],
                in_recv.at[f, m],
                in_ss.at[df, dm],
                in_rs.at[df, dm],
                in_group(df, dm),
            )
        )
    sums = []
    for dc, df in wide:
        sums.append(
            send(g_send, g_recv.at[c, f], g_ss.at[dc, df], g_rs.at[dc, df], in_wide(dc, df))
        )
    b_recv[f] = b_send[f]
    in_recv[f, m] = in_send[f]
    g_recv[c, f] = g_send[...]
    for copy in flying:
        copy.wait()

    total = sq_recv[f, 0]
    for other in range(1, mps):
        total = total + sq_recv[f, other]
    inverse_table = lax.rsqrt(total / total_width + epsilon)
    inner_rows = []
    for j in range(tiles):
        rows = in_recv[j, 0]
        for other in range(1, mps):
            rows = rows + in_recv[j, other]
        inner_rows.append(rows)
    factors = []
    for s in range(tiles):
        row = inner_rows[s][0:1]
        for j in range(tiles):
            row = row + reads(j, s) * inner_rows[j][1:2]
        inverse = to_column(inverse_table[2 + s : 3 + s])
        inner = to_column(row)
        factors.append((inverse, inverse * inverse * inverse * (inner / total_width)))

    def backward_head(h, carry):
        cols = head_cols(h)
        blocks = [b_recv[j, :, cols].astype(F32) for j in range(tiles)]
        parts = []
        for s in range(tiles):
            grad = blocks[s][:tt]
            for j in range(tiles):
                grad = grad + reads(j, s) * blocks[j][tt:]
            inverse, factor = factors[s]
            parts.append(inverse * grad - sp_sc[s * tt : (s + 1) * tt, cols] * factor)
        upstream = jnp.concatenate(parts, axis=0).astype(BF16)
        weights = p_sc[h]
        grad_weights = dot_nt(upstream, v_ref[:, cols])
        inner = jnp.sum(weights * grad_weights, axis=-1, keepdims=True)
        grad_scores = (weights * (grad_weights - inner) * scale).astype(BF16)
        gq_ref[:, cols] = dot_nn(grad_scores, k_ref[:, cols]).astype(BF16)
        gk_ref[:, cols] = dot_tn(grad_scores, q_ref[:, cols]).astype(BF16)
        gv_ref[:, cols] = dot_tn(weights.astype(BF16), upstream).astype(BF16)
        return carry

    each_head(backward_head, 0)

    for copy in sums:
        copy.wait()
    total = None
    for other in range(clips):
        for t in range(frames):
            total = g_recv[other, t] if total is None else total + g_recv[other, t]
    for g in range(3):
        for h in range(heads):
            row = g * heads + h
            gg_ref[g : g + 1, h * HD : (h + 1) * HD] = total[row : row + 1]


def write_out(*refs):
    sems = refs[10]
    copies = [pltpu.make_async_copy(refs[i], refs[5 + i], sems.at[i]) for i in range(5)]
    for copy in copies:
        copy.start()
    for copy in copies:
        copy.wait()


def body(sizes, query, key, value, gains, warp_lists, cotangent):
    clips, frames, mps = sizes
    tiles, tt, width = query.shape[2:]
    heads = width // HD
    count = tiles * tt
    dims = (clips, frames, mps, tiles, tt, heads)
    vmem = pl.BlockSpec(memory_space=pltpu.VMEM)
    table = pad8(tiles + 2)
    gain_rows = pad8(3 * heads)
    dma = pltpu.SemaphoreType.DMA
    results = [((frames * tt, width), BF16)] + [((count, width), BF16)] * 3 + [((3, width), F32)]
    outs = pl.pallas_call(
        functools.partial(kernel, dims),
        out_shape=tuple(pltpu.VMEM(shape, kind) for shape, kind in results),
        in_specs=[vmem, vmem, vmem, vmem, pl.BlockSpec(memory_space=pltpu.SMEM), vmem],
        out_specs=(vmem,) * 5,
        scratch_shapes=[
            pltpu.VMEM((heads, count, count), F32),
            pltpu.VMEM((count, width), F32),
            pltpu.VMEM((pad8(tiles), HD), F32),
            pltpu.VMEM((frames, 2 * tt, width), BF16),
            pltpu.VMEM((frames, 2 * tt, width), BF16),
            pltpu.VMEM((frames, table, HD), F32),
            pltpu.VMEM((frames, mps, table, HD), F32),
            pltpu.VMEM((frames, 2 * tt, width), BF16),
            pltpu.VMEM((frames, 2 * tt, width), BF16),
            pltpu.VMEM((frames, 8, HD), F32),
            pltpu.VMEM((frames, mps, 8, HD), F32),
            pltpu.VMEM((gain_rows, HD), F32),
            pltpu.VMEM((clips, frames, gain_rows, HD), F32),
            dma((frames,)),
            dma((frames,)),
            dma((frames, mps)),
            dma((frames, mps)),
            dma((frames,)),
            dma((frames,)),
            dma((frames, mps)),
            dma((frames, mps)),
            dma((clips, frames)),
            dma((clips, frames)),
        ],
        compiler_params=pltpu.CompilerParams(
            collective_id=0, has_side_effects=True, vmem_limit_bytes=56 * 2**20
        ),
    )(
        query.reshape(count, width),
        key.reshape(count, width),
        value.reshape(count, width),
        gains,
        warp_lists.reshape(tiles),
        cotangent.reshape(frames * tt, width),
    )
    outs = pl.pallas_call(
        write_out,
        out_shape=tuple(jax.ShapeDtypeStruct(shape, kind) for shape, kind in results),
        in_specs=[vmem] * 5,
        out_specs=(pl.BlockSpec(memory_space=pl.ANY),) * 5,
        scratch_shapes=[dma((5,))],
    )(*(pltpu.with_memory_space_constraint(out, pltpu.VMEM) for out in outs))
    temporal, back_q, back_k, back_v, grad_gains = outs
    return (
        temporal.reshape(cotangent.shape),
        back_q.reshape(query.shape),
        back_k.reshape(query.shape),
        back_v.reshape(query.shape),
        grad_gains,
    )


def solution(mesh):
    sizes = (mesh.shape["clip"], mesh.shape["frame"], mesh.shape["mp"])
    return jax.shard_map(
        functools.partial(body, sizes),
        mesh=mesh,
        in_specs=(
            P("clip", "frame", None, None, "mp"),
            P("clip", "frame", None, None, "mp"),
            P("clip", "frame", None, None, "mp"),
            P(None, "mp"),
            P("clip", "frame", None),
            P("clip", None, "frame", None, "mp"),
        ),
        out_specs=(
            P("clip", None, "frame", None, "mp"),
            P("clip", "frame", None, None, "mp"),
            P("clip", "frame", None, None, "mp"),
            P("clip", "frame", None, None, "mp"),
            P(None, "mp"),
        ),
        check_vma=False,
    )
```

```python
import functools
import math

import jax
import jax.numpy as jnp
from jax import lax
from jax.experimental import pallas as pl
from jax.experimental.pallas import tpu as pltpu
from jax.sharding import PartitionSpec as P

HD = 128
MESH = pl.DeviceIdType.MESH
epsilon = 1e-06
F32 = jnp.float32
BF16 = jnp.bfloat16


def pad8(n):
    return (n + 7) // 8 * 8


def cuts(heads):
    middle = (heads + 1) // 2
    return [(0, middle), (middle, heads)]


def dot_nt(a, b):
    return lax.dot_general(a, b, (((1,), (1,)), ((), ())), preferred_element_type=F32)


def dot_nn(a, b):
    return lax.dot_general(a, b, (((1,), (0,)), ((), ())), preferred_element_type=F32)


def dot_tn(a, b):
    return lax.dot_general(a, b, (((0,), (0,)), ((), ())), preferred_element_type=F32)


def softmax(scores, scale):
    top = jnp.max(scores, axis=0, keepdims=True)
    expon = jnp.exp((scores - top) * scale)
    return expon * (1.0 / jnp.sum(expon, axis=0, keepdims=True))


def kernel(
    dims,
    q_ref,
    k_ref,
    v_ref,
    gains_ref,
    warp_ref,
    cot_ref,
    tout_ref,
    gq_ref,
    gk_ref,
    gv_ref,
    gg_ref,
    p_sc,
    sp_sc,
    table_sc,
    a_send,
    a_recv,
    sq_send,
    sq_recv,
    b_send,
    b_recv,
    in_send,
    in_recv,
    g_send,
    g_recv,
    a_ss,
    a_rs,
    sq_ss,
    sq_rs,
    b_ss,
    b_rs,
    in_ss,
    in_rs,
    g_ss,
    g_rs,
):
    clips, frames, mps, tiles, tt, heads = dims
    total_width = float(heads * HD * mps)
    scale = 1.0 / math.sqrt(HD)
    c = lax.axis_index("clip")
    f = lax.axis_index("frame")
    m = lax.axis_index("mp")

    def at(index, step, size):
        return lax.rem(index + step, size) if step else index

    groups = cuts(heads)
    group = [(df, dm) for df in range(frames) for dm in range(mps) if (df, dm) != (0, 0)]
    wide = [(dc, df) for dc in range(clips) for df in range(frames) if (dc, df) != (0, 0)]

    def in_group(df, dm):
        return {"frame": at(f, df, frames), "mp": at(m, dm, mps)}

    def in_wide(dc, df):
        return {"clip": at(c, dc, clips), "frame": at(f, df, frames)}

    barrier = pltpu.get_barrier_semaphore()
    peers = [in_group(*step) for step in group]
    peers += [in_wide(dc, df) for dc, df in wide if dc]
    for peer in peers:
        pl.semaphore_signal(barrier, inc=1, device_id=peer, device_id_type=MESH)

    def head_cols(h):
        if isinstance(h, int):
            return slice(h * HD, (h + 1) * HD)
        return pl.ds(pl.multiple_of(h * HD, HD), HD)

    def each_head(fn, carry, low=0, high=heads):
        if tiles * tt <= 128:
            for h in range(low, high):
                carry = fn(h, carry)
            return carry
        return lax.fori_loop(low, high, fn, carry)

    def send(src, dst, send_sem, recv_sem, peer):
        copy = pltpu.make_async_remote_copy(
            src_ref=src,
            dst_ref=dst,
            send_sem=send_sem,
            recv_sem=recv_sem,
            device_id=peer,
            device_id_type=MESH,
        )
        copy.start()
        return copy

    diagonal = lax.broadcasted_iota(jnp.int32, (tt, HD), 0) == lax.broadcasted_iota(
        jnp.int32, (tt, HD), 1
    )

    def to_row(column):
        return jnp.sum(jnp.where(diagonal, column, 0.0), axis=0, keepdims=True)

    def to_column(row):
        return jnp.sum(jnp.where(diagonal, row, 0.0), axis=1, keepdims=True)

    def spatial_head(h, squares):
        cols = head_cols(h)
        weights = softmax(dot_nt(k_ref[:, cols], q_ref[:, cols]), scale)
        p_sc[h] = weights
        out = dot_tn(weights.astype(BF16), v_ref[:, cols]).astype(BF16).astype(F32)
        sp_sc[:, cols] = out
        return squares + out * out

    def reads(j, s):
        return jnp.where(jnp.full((1, HD), warp_ref[j], jnp.int32) == s, 1.0, 0.0)

    def tile_pair(ref, j, low, high):
        picks = [reads(j, s) for s in range(tiles)]

        def one_head(h, carry):
            cols = head_cols(h)
            own = sp_sc[pl.ds(pl.multiple_of(j * tt, 8), tt), cols]
            source = picks[0] * sp_sc[0:tt, cols]
            for s in range(1, tiles):
                source = source + picks[s] * sp_sc[s * tt : (s + 1) * tt, cols]
            ref[h] = jnp.concatenate([own, source], axis=0).astype(BF16)
            return carry

        each_head(one_head, 0, low, high)

    def square_rows(ref, j):
        source = reads(j, 0) * table_sc[0:1, :]
        for s in range(1, tiles):
            source = source + reads(j, s) * table_sc[s : s + 1, :]
        ref[0:1, :] = table_sc[pl.ds(j, 1), :]
        ref[1:2, :] = source
        ref[2 : 2 + tiles, :] = table_sc[0:tiles, :]

    flying = []
    squares = jnp.zeros((tiles * tt, HD), F32)
    for part, (low, high) in enumerate(groups):
        squares = each_head(spatial_head, squares, low, high)
        if part == 0:
            pl.semaphore_wait(barrier, len(peers))
        for df in range(1, frames):
            j = at(f, df, frames)
            tile_pair(a_send.at[df], j, low, high)
            flying.append(
                send(
                    a_send.at[df, low:high],
                    a_recv.at[f, low:high],
                    a_ss.at[df, part],
                    a_rs.at[df, part],
                    {"frame": j},
                )
            )
    square_sum = jnp.sum(squares, axis=1, keepdims=True)
    for s in range(tiles):
        table_sc[pl.ds(s, 1), :] = to_row(square_sum[s * tt : (s + 1) * tt])
    for df in range(frames):
        square_rows(sq_send.at[df], at(f, df, frames))
    for df, dm in reversed(group):
        flying.append(
            send(
                sq_send.at[df],
                sq_recv.at[f, m],
                sq_ss.at[df, dm],
                sq_rs.at[df, dm],
                in_group(df, dm),
            )
        )
    tile_pair(a_recv.at[f], f, 0, heads)
    sq_recv[f, m] = sq_send[0]
    for copy in flying:
        copy.wait_recv()
    sent = flying

    inverse_rows = []
    for t in range(frames):
        total = sq_recv[t, 0]
        for other in range(1, mps):
            total = total + sq_recv[t, other]
        inverse_rows.append(lax.rsqrt(total / total_width + epsilon))
    inverse_own = jnp.concatenate([to_column(rows[0:1]) for rows in inverse_rows], axis=0)
    inverse_source = jnp.concatenate([to_column(rows[1:2]) for rows in inverse_rows], axis=0)
    count = frames * tt
    frame_k = lax.broadcasted_iota(jnp.int32, (count, count), 0) // tt
    frame_q = lax.broadcasted_iota(jnp.int32, (count, count), 1) // tt
    causal = frame_q >= frame_k

    def temporal_head(h, carry):
        dot_own, dot_source = carry
        cols = head_cols(h)
        blocks = [a_recv[t, h].astype(F32) for t in range(frames)]
        own = jnp.concatenate([block[:tt] for block in blocks], axis=0)
        source = jnp.concatenate([block[tt:] for block in blocks], axis=0)
        normed = (own * inverse_own).astype(BF16).astype(F32)
        warped = (source * inverse_source).astype(BF16).astype(F32)
        gain_q = gains_ref[0:1, cols]
        gain_k = gains_ref[1:2, cols]
        gain_v = gains_ref[2:3, cols]
        tq = (normed * gain_q).astype(BF16)
        tk = (warped * gain_k).astype(BF16)
        tv = (warped * gain_v).astype(BF16)
        weights = softmax(jnp.where(causal, dot_nt(tk, tq), -1e30), scale)
        rounded = weights.astype(BF16)
        tout_ref[:, cols] = dot_tn(rounded, tv).astype(BF16)
        upstream = cot_ref[:, cols]
        grad_weights = dot_nt(tv, upstream)
        inner = jnp.sum(weights * grad_weights, axis=0, keepdims=True)
        grad_scores = (weights * (grad_weights - inner) * scale).astype(BF16)
        dq = dot_tn(grad_scores, tk).astype(BF16).astype(F32)
        dk = dot_nn(grad_scores, tq).astype(BF16).astype(F32)
        dv = dot_nn(rounded, upstream).astype(BF16).astype(F32)
        direct = (dq * gain_q).astype(BF16).astype(F32)
        moved = (dk * gain_k + dv * gain_v).astype(BF16).astype(F32)
        for t in range(frames):
            rows = slice(t * tt, (t + 1) * tt)
            b_send[t, h] = jnp.concatenate([direct[rows], moved[rows]], axis=0).astype(BF16)
        g_send[pl.ds(h, 1), :] = jnp.sum(dq * normed, axis=0, keepdims=True)
        g_send[pl.ds(heads + h, 1), :] = jnp.sum(dk * warped, axis=0, keepdims=True)
        g_send[pl.ds(2 * heads + h, 1), :] = jnp.sum(dv * warped, axis=0, keepdims=True)
        return dot_own + direct * own, dot_source + moved * source

    zero = jnp.zeros((count, HD), F32)
    flying = []
    carry = (zero, zero)
    for part, (low, high) in enumerate(groups):
        carry = each_head(temporal_head, carry, low, high)
        for df in range(1, frames):
            t = at(f, df, frames)
            flying.append(
                send(
                    b_send.at[t, low:high],
                    b_recv.at[f, low:high],
                    b_ss.at[df, part],
                    b_rs.at[df, part],
                    {"frame": t},
                )
            )
    dot_own, dot_source = carry
    dot_own = jnp.sum(dot_own, axis=1, keepdims=True)
    dot_source = jnp.sum(dot_source, axis=1, keepdims=True)
    for t in range(frames):
        rows = slice(t * tt, (t + 1) * tt)
        in_send[t, 0:1, :] = to_row(dot_own[rows])
        in_send[t, 1:2, :] = to_row(dot_source[rows])
    for df, dm in group:
        flying.append(
            send(
                in_send.at[at(f, df, frames)],
                in_recv.at[f, m],
                in_ss.at[df, dm],
                in_rs.at[df, dm],
                in_group(df, dm),
            )
        )
    sums = []
    for dc, df in wide:
        sums.append(
            send(g_send, g_recv.at[c, f], g_ss.at[dc, df], g_rs.at[dc, df], in_wide(dc, df))
        )
    b_recv[f] = b_send[f]
    in_recv[f, m] = in_send[f]
    g_recv[c, f] = g_send[...]
    for copy in flying:
        copy.wait_recv()
    sent = sent + flying + sums

    total = sq_recv[f, 0]
    for other in range(1, mps):
        total = total + sq_recv[f, other]
    inverse_table = lax.rsqrt(total / total_width + epsilon)
    inner_rows = []
    for j in range(tiles):
        rows = in_recv[j, 0]
        for other in range(1, mps):
            rows = rows + in_recv[j, other]
        inner_rows.append(rows)
    factors = []
    for s in range(tiles):
        row = inner_rows[s][0:1]
        for j in range(tiles):
            row = row + reads(j, s) * inner_rows[j][1:2]
        inverse = to_column(inverse_table[2 + s : 3 + s])
        inner = to_column(row)
        factors.append((inverse, inverse * inverse * inverse * (inner / total_width)))

    def backward_head(h, carry):
        cols = head_cols(h)
        blocks = [b_recv[j, h].astype(F32) for j in range(tiles)]
        parts = []
        for s in range(tiles):
            grad = blocks[s][:tt]
            for j in range(tiles):
                grad = grad + reads(j, s) * blocks[j][tt:]
            inverse, factor = factors[s]
            parts.append(inverse * grad - sp_sc[s * tt : (s + 1) * tt, cols] * factor)
        upstream = jnp.concatenate(parts, axis=0).astype(BF16)
        weights = p_sc[h]
        grad_weights = dot_nt(v_ref[:, cols], upstream)
        inner = jnp.sum(weights * grad_weights, axis=0, keepdims=True)
        grad_scores = (weights * (grad_weights - inner) * scale).astype(BF16)
        gq_ref[:, cols] = dot_tn(grad_scores, k_ref[:, cols]).astype(BF16)
        gk_ref[:, cols] = dot_nn(grad_scores, q_ref[:, cols]).astype(BF16)
        gv_ref[:, cols] = dot_nn(weights.astype(BF16), upstream).astype(BF16)
        return carry

    each_head(backward_head, 0)

    for copy in sums:
        copy.wait_recv()
    total = None
    for other in range(clips):
        for t in range(frames):
            total = g_recv[other, t] if total is None else total + g_recv[other, t]
    for g in range(3):
        for h in range(heads):
            row = g * heads + h
            gg_ref[g : g + 1, h * HD : (h + 1) * HD] = total[row : row + 1]
    for copy in sent:
        copy.wait_send()


def write_out(*refs):
    sems = refs[10]
    copies = [pltpu.make_async_copy(refs[i], refs[5 + i], sems.at[i]) for i in range(5)]
    for copy in copies:
        copy.start()
    for copy in copies:
        copy.wait()


def body(sizes, query, key, value, gains, warp_lists, cotangent):
    clips, frames, mps = sizes
    tiles, tt, width = query.shape[2:]
    heads = width // HD
    count = tiles * tt
    dims = (clips, frames, mps, tiles, tt, heads)
    vmem = pl.BlockSpec(memory_space=pltpu.VMEM)
    table = pad8(tiles + 2)
    gain_rows = pad8(3 * heads)
    dma = pltpu.SemaphoreType.DMA
    parts = len(cuts(heads))
    results = [((frames * tt, width), BF16)] + [((count, width), BF16)] * 3 + [((3, width), F32)]
    outs = pl.pallas_call(
        functools.partial(kernel, dims),
        out_shape=tuple(pltpu.VMEM(shape, kind) for shape, kind in results),
        in_specs=[vmem, vmem, vmem, vmem, pl.BlockSpec(memory_space=pltpu.SMEM), vmem],
        out_specs=(vmem,) * 5,
        scratch_shapes=[
            pltpu.VMEM((heads, count, count), F32),
            pltpu.VMEM((count, width), F32),
            pltpu.VMEM((pad8(tiles), HD), F32),
            pltpu.VMEM((frames, heads, 2 * tt, HD), BF16),
            pltpu.VMEM((frames, heads, 2 * tt, HD), BF16),
            pltpu.VMEM((frames, table, HD), F32),
            pltpu.VMEM((frames, mps, table, HD), F32),
            pltpu.VMEM((frames, heads, 2 * tt, HD), BF16),
            pltpu.VMEM((frames, heads, 2 * tt, HD), BF16),
            pltpu.VMEM((frames, 8, HD), F32),
            pltpu.VMEM((frames, mps, 8, HD), F32),
            pltpu.VMEM((gain_rows, HD), F32),
            pltpu.VMEM((clips, frames, gain_rows, HD), F32),
            dma((frames, parts)),
            dma((frames, parts)),
            dma((frames, mps)),
            dma((frames, mps)),
            dma((frames, parts)),
            dma((frames, parts)),
            dma((frames, mps)),
            dma((frames, mps)),
            dma((clips, frames)),
            dma((clips, frames)),
        ],
        compiler_params=pltpu.CompilerParams(
            collective_id=0, has_side_effects=True, vmem_limit_bytes=56 * 2**20
        ),
    )(
        query.reshape(count, width),
        key.reshape(count, width),
        value.reshape(count, width),
        gains,
        warp_lists.reshape(tiles),
        cotangent.reshape(frames * tt, width),
    )
    outs = pl.pallas_call(
        write_out,
        out_shape=tuple(jax.ShapeDtypeStruct(shape, kind) for shape, kind in results),
        in_specs=[vmem] * 5,
        out_specs=(pl.BlockSpec(memory_space=pl.ANY),) * 5,
        scratch_shapes=[dma((5,))],
    )(*(pltpu.with_memory_space_constraint(out, pltpu.VMEM) for out in outs))
    temporal, back_q, back_k, back_v, grad_gains = outs
    return (
        temporal.reshape(cotangent.shape),
        back_q.reshape(query.shape),
        back_k.reshape(query.shape),
        back_v.reshape(query.shape),
        grad_gains,
    )


def solution(mesh):
    sizes = (mesh.shape["clip"], mesh.shape["frame"], mesh.shape["mp"])
    return jax.shard_map(
        functools.partial(body, sizes),
        mesh=mesh,
        in_specs=(
            P("clip", "frame", None, None, "mp"),
            P("clip", "frame", None, None, "mp"),
            P("clip", "frame", None, None, "mp"),
            P(None, "mp"),
            P("clip", "frame", None),
            P("clip", None, "frame", None, "mp"),
        ),
        out_specs=(
            P("clip", None, "frame", None, "mp"),
            P("clip", "frame", None, None, "mp"),
            P("clip", "frame", None, None, "mp"),
            P("clip", "frame", None, None, "mp"),
            P(None, "mp"),
        ),
        check_vma=False,
    )
```

```python
import functools
import math

import jax
import jax.numpy as jnp
from jax import lax
from jax.experimental import pallas as pl
from jax.experimental.pallas import tpu as pltpu
from jax.sharding import PartitionSpec as P

HD = 128
MESH = pl.DeviceIdType.MESH
epsilon = 1e-06
F32 = jnp.float32
BF16 = jnp.bfloat16


def pad8(n):
    return (n + 7) // 8 * 8


def cuts(heads):
    middle = (heads + 1) // 2
    return [(0, middle), (middle, heads)]


def dot_nt(a, b):
    return lax.dot_general(a, b, (((1,), (1,)), ((), ())), preferred_element_type=F32)


def dot_nn(a, b):
    return lax.dot_general(a, b, (((1,), (0,)), ((), ())), preferred_element_type=F32)


def dot_tn(a, b):
    return lax.dot_general(a, b, (((0,), (0,)), ((), ())), preferred_element_type=F32)


def softmax(scores, scale):
    top = jnp.max(scores, axis=0, keepdims=True)
    expon = jnp.exp((scores - top) * scale)
    return expon * (1.0 / jnp.sum(expon, axis=0, keepdims=True))


def kernel(
    dims,
    q_in,
    k_in,
    v_in,
    gains_in,
    warp_ref,
    cot_in,
    tout_ref,
    gq_ref,
    gk_ref,
    gv_ref,
    gg_ref,
    q_ref,
    k_ref,
    v_ref,
    gains_ref,
    cot_ref,
    p_sc,
    sp_sc,
    table_sc,
    a_send,
    a_recv,
    sq_send,
    sq_recv,
    b_send,
    b_recv,
    in_send,
    in_recv,
    g_send,
    g_recv,
    a_ss,
    a_rs,
    sq_ss,
    sq_rs,
    b_ss,
    b_rs,
    in_ss,
    in_rs,
    g_ss,
    g_rs,
    load_sems,
):
    clips, frames, mps, tiles, tt, heads = dims
    total_width = float(heads * HD * mps)
    scale = 1.0 / math.sqrt(HD)
    c = lax.axis_index("clip")
    f = lax.axis_index("frame")
    m = lax.axis_index("mp")

    def at(index, step, size):
        return lax.rem(index + step, size) if step else index

    groups = cuts(heads)
    group = [(df, dm) for df in range(frames) for dm in range(mps) if (df, dm) != (0, 0)]
    wide = [(dc, df) for dc in range(clips) for df in range(frames) if (dc, df) != (0, 0)]

    def in_group(df, dm):
        return {"frame": at(f, df, frames), "mp": at(m, dm, mps)}

    def in_wide(dc, df):
        return {"clip": at(c, dc, clips), "frame": at(f, df, frames)}

    pairs = [(q_in, q_ref), (k_in, k_ref), (v_in, v_ref), (gains_in, gains_ref), (cot_in, cot_ref)]
    loads = [pltpu.make_async_copy(*pair, load_sems.at[i]) for i, pair in enumerate(pairs)]
    for load in loads:
        load.start()
    barrier = pltpu.get_barrier_semaphore()
    peers = [in_group(*step) for step in group]
    peers += [in_wide(dc, df) for dc, df in wide if dc]
    for peer in peers:
        pl.semaphore_signal(barrier, inc=1, device_id=peer, device_id_type=MESH)

    def head_cols(h):
        if isinstance(h, int):
            return slice(h * HD, (h + 1) * HD)
        return pl.ds(pl.multiple_of(h * HD, HD), HD)

    def each_head(fn, carry, low=0, high=heads):
        if tiles * tt <= 128:
            for h in range(low, high):
                carry = fn(h, carry)
            return carry
        return lax.fori_loop(low, high, fn, carry)

    def send(src, dst, send_sem, recv_sem, peer):
        copy = pltpu.make_async_remote_copy(
            src_ref=src,
            dst_ref=dst,
            send_sem=send_sem,
            recv_sem=recv_sem,
            device_id=peer,
            device_id_type=MESH,
        )
        copy.start()
        return copy

    diagonal = lax.broadcasted_iota(jnp.int32, (tt, HD), 0) == lax.broadcasted_iota(
        jnp.int32, (tt, HD), 1
    )

    def to_row(column):
        return jnp.sum(jnp.where(diagonal, column, 0.0), axis=0, keepdims=True)

    def to_column(row):
        return jnp.sum(jnp.where(diagonal, row, 0.0), axis=1, keepdims=True)

    def spatial_head(h, squares):
        cols = head_cols(h)
        weights = softmax(dot_nt(k_ref[:, cols], q_ref[:, cols]), scale)
        p_sc[h] = weights
        out = dot_tn(weights.astype(BF16), v_ref[:, cols]).astype(BF16).astype(F32)
        sp_sc[:, cols] = out
        return squares + out * out

    def reads(j, s):
        return jnp.where(jnp.full((1, HD), warp_ref[j], jnp.int32) == s, 1.0, 0.0)

    def tile_pair(ref, j, low, high):
        picks = [reads(j, s) for s in range(tiles)]

        def one_head(h, carry):
            cols = head_cols(h)
            own = sp_sc[pl.ds(pl.multiple_of(j * tt, 8), tt), cols]
            source = picks[0] * sp_sc[0:tt, cols]
            for s in range(1, tiles):
                source = source + picks[s] * sp_sc[s * tt : (s + 1) * tt, cols]
            ref[h] = jnp.concatenate([own, source], axis=0).astype(BF16)
            return carry

        each_head(one_head, 0, low, high)

    def square_rows(ref, j):
        source = reads(j, 0) * table_sc[0:1, :]
        for s in range(1, tiles):
            source = source + reads(j, s) * table_sc[s : s + 1, :]
        ref[0:1, :] = table_sc[pl.ds(j, 1), :]
        ref[1:2, :] = source
        ref[2 : 2 + tiles, :] = table_sc[0:tiles, :]

    for load in loads[:3]:
        load.wait()
    flying = []
    squares = jnp.zeros((tiles * tt, HD), F32)
    for part, (low, high) in enumerate(groups):
        squares = each_head(spatial_head, squares, low, high)
        if part == 0:
            pl.semaphore_wait(barrier, len(peers))
        for df in range(1, frames):
            j = at(f, df, frames)
            tile_pair(a_send.at[df], j, low, high)
            flying.append(
                send(
                    a_send.at[df, low:high],
                    a_recv.at[f, low:high],
                    a_ss.at[df, part],
                    a_rs.at[df, part],
                    {"frame": j},
                )
            )
    square_sum = jnp.sum(squares, axis=1, keepdims=True)
    for s in range(tiles):
        table_sc[pl.ds(s, 1), :] = to_row(square_sum[s * tt : (s + 1) * tt])
    for df in range(frames):
        square_rows(sq_send.at[df], at(f, df, frames))
    for df, dm in reversed(group):
        flying.append(
            send(
                sq_send.at[df],
                sq_recv.at[f, m],
                sq_ss.at[df, dm],
                sq_rs.at[df, dm],
                in_group(df, dm),
            )
        )
    tile_pair(a_recv.at[f], f, 0, heads)
    sq_recv[f, m] = sq_send[0]
    for load in loads[3:]:
        load.wait()
    for copy in flying:
        copy.wait_recv()
    sent = flying

    inverse_rows = []
    for t in range(frames):
        total = sq_recv[t, 0]
        for other in range(1, mps):
            total = total + sq_recv[t, other]
        inverse_rows.append(lax.rsqrt(total / total_width + epsilon))
    inverse_own = jnp.concatenate([to_column(rows[0:1]) for rows in inverse_rows], axis=0)
    inverse_source = jnp.concatenate([to_column(rows[1:2]) for rows in inverse_rows], axis=0)
    count = frames * tt
    frame_k = lax.broadcasted_iota(jnp.int32, (count, count), 0) // tt
    frame_q = lax.broadcasted_iota(jnp.int32, (count, count), 1) // tt
    causal = frame_q >= frame_k

    def temporal_head(h, carry):
        dot_own, dot_source = carry
        cols = head_cols(h)
        blocks = [a_recv[t, h].astype(F32) for t in range(frames)]
        own = jnp.concatenate([block[:tt] for block in blocks], axis=0)
        source = jnp.concatenate([block[tt:] for block in blocks], axis=0)
        normed = (own * inverse_own).astype(BF16).astype(F32)
        warped = (source * inverse_source).astype(BF16).astype(F32)
        gain_q = gains_ref[0:1, cols]
        gain_k = gains_ref[1:2, cols]
        gain_v = gains_ref[2:3, cols]
        tq = (normed * gain_q).astype(BF16)
        tk = (warped * gain_k).astype(BF16)
        tv = (warped * gain_v).astype(BF16)
        weights = softmax(jnp.where(causal, dot_nt(tk, tq), -1e30), scale)
        rounded = weights.astype(BF16)
        tout_ref[:, cols] = dot_tn(rounded, tv).astype(BF16)
        upstream = cot_ref[:, cols]
        grad_weights = dot_nt(tv, upstream)
        inner = jnp.sum(weights * grad_weights, axis=0, keepdims=True)
        grad_scores = (weights * (grad_weights - inner) * scale).astype(BF16)
        dq = dot_tn(grad_scores, tk).astype(BF16).astype(F32)
        dk = dot_nn(grad_scores, tq).astype(BF16).astype(F32)
        dv = dot_nn(rounded, upstream).astype(BF16).astype(F32)
        direct = (dq * gain_q).astype(BF16).astype(F32)
        moved = (dk * gain_k + dv * gain_v).astype(BF16).astype(F32)
        for t in range(frames):
            rows = slice(t * tt, (t + 1) * tt)
            b_send[t, h] = jnp.concatenate([direct[rows], moved[rows]], axis=0).astype(BF16)
        g_send[pl.ds(h, 1), :] = jnp.sum(dq * normed, axis=0, keepdims=True)
        g_send[pl.ds(heads + h, 1), :] = jnp.sum(dk * warped, axis=0, keepdims=True)
        g_send[pl.ds(2 * heads + h, 1), :] = jnp.sum(dv * warped, axis=0, keepdims=True)
        return dot_own + direct * own, dot_source + moved * source

    zero = jnp.zeros((count, HD), F32)
    flying = []
    carry = (zero, zero)
    for part, (low, high) in enumerate(groups):
        carry = each_head(temporal_head, carry, low, high)
        for df in range(1, frames):
            t = at(f, df, frames)
            flying.append(
                send(
                    b_send.at[t, low:high],
                    b_recv.at[f, low:high],
                    b_ss.at[df, part],
                    b_rs.at[df, part],
                    {"frame": t},
                )
            )
    dot_own, dot_source = carry
    dot_own = jnp.sum(dot_own, axis=1, keepdims=True)
    dot_source = jnp.sum(dot_source, axis=1, keepdims=True)
    for t in range(frames):
        rows = slice(t * tt, (t + 1) * tt)
        in_send[t, 0:1, :] = to_row(dot_own[rows])
        in_send[t, 1:2, :] = to_row(dot_source[rows])
    for df, dm in group:
        flying.append(
            send(
                in_send.at[at(f, df, frames)],
                in_recv.at[f, m],
                in_ss.at[df, dm],
                in_rs.at[df, dm],
                in_group(df, dm),
            )
        )
    sums = []
    for dc, df in wide:
        sums.append(
            send(g_send, g_recv.at[c, f], g_ss.at[dc, df], g_rs.at[dc, df], in_wide(dc, df))
        )
    b_recv[f] = b_send[f]
    in_recv[f, m] = in_send[f]
    g_recv[c, f] = g_send[...]
    for copy in flying:
        copy.wait_recv()
    sent = sent + flying + sums

    total = sq_recv[f, 0]
    for other in range(1, mps):
        total = total + sq_recv[f, other]
    inverse_table = lax.rsqrt(total / total_width + epsilon)
    inner_rows = []
    for j in range(tiles):
        rows = in_recv[j, 0]
        for other in range(1, mps):
            rows = rows + in_recv[j, other]
        inner_rows.append(rows)
    factors = []
    for s in range(tiles):
        row = inner_rows[s][0:1]
        for j in range(tiles):
            row = row + reads(j, s) * inner_rows[j][1:2]
        inverse = to_column(inverse_table[2 + s : 3 + s])
        inner = to_column(row)
        factors.append((inverse, inverse * inverse * inverse * (inner / total_width)))

    def backward_head(h, carry):
        cols = head_cols(h)
        blocks = [b_recv[j, h].astype(F32) for j in range(tiles)]
        parts = []
        for s in range(tiles):
            grad = blocks[s][:tt]
            for j in range(tiles):
                grad = grad + reads(j, s) * blocks[j][tt:]
            inverse, factor = factors[s]
            parts.append(inverse * grad - sp_sc[s * tt : (s + 1) * tt, cols] * factor)
        upstream = jnp.concatenate(parts, axis=0).astype(BF16)
        weights = p_sc[h]
        grad_weights = dot_nt(v_ref[:, cols], upstream)
        inner = jnp.sum(weights * grad_weights, axis=0, keepdims=True)
        grad_scores = (weights * (grad_weights - inner) * scale).astype(BF16)
        gq_ref[:, cols] = dot_tn(grad_scores, k_ref[:, cols]).astype(BF16)
        gk_ref[:, cols] = dot_nn(grad_scores, q_ref[:, cols]).astype(BF16)
        gv_ref[:, cols] = dot_nn(weights.astype(BF16), upstream).astype(BF16)
        return carry

    each_head(backward_head, 0)

    for copy in sums:
        copy.wait_recv()
    total = None
    for other in range(clips):
        for t in range(frames):
            total = g_recv[other, t] if total is None else total + g_recv[other, t]
    for g in range(3):
        for h in range(heads):
            row = g * heads + h
            gg_ref[g : g + 1, h * HD : (h + 1) * HD] = total[row : row + 1]
    for copy in sent:
        copy.wait_send()


def write_out(*refs):
    sems = refs[10]
    copies = [pltpu.make_async_copy(refs[i], refs[5 + i], sems.at[i]) for i in range(5)]
    for copy in copies:
        copy.start()
    for copy in copies:
        copy.wait()


def body(sizes, query, key, value, gains, warp_lists, cotangent):
    clips, frames, mps = sizes
    tiles, tt, width = query.shape[2:]
    heads = width // HD
    count = tiles * tt
    dims = (clips, frames, mps, tiles, tt, heads)
    vmem = pl.BlockSpec(memory_space=pltpu.VMEM)
    far = pl.BlockSpec(memory_space=pl.ANY)
    table = pad8(tiles + 2)
    gain_rows = pad8(3 * heads)
    dma = pltpu.SemaphoreType.DMA
    parts = len(cuts(heads))
    results = [((frames * tt, width), BF16)] + [((count, width), BF16)] * 3 + [((3, width), F32)]
    outs = pl.pallas_call(
        functools.partial(kernel, dims),
        out_shape=tuple(pltpu.VMEM(shape, kind) for shape, kind in results),
        in_specs=[far, far, far, far, pl.BlockSpec(memory_space=pltpu.SMEM), far],
        out_specs=(vmem,) * 5,
        scratch_shapes=[
            pltpu.VMEM((count, width), BF16),
            pltpu.VMEM((count, width), BF16),
            pltpu.VMEM((count, width), BF16),
            pltpu.VMEM((3, width), F32),
            pltpu.VMEM((frames * tt, width), BF16),
            pltpu.VMEM((heads, count, count), F32),
            pltpu.VMEM((count, width), F32),
            pltpu.VMEM((pad8(tiles), HD), F32),
            pltpu.VMEM((frames, heads, 2 * tt, HD), BF16),
            pltpu.VMEM((frames, heads, 2 * tt, HD), BF16),
            pltpu.VMEM((frames, table, HD), F32),
            pltpu.VMEM((frames, mps, table, HD), F32),
            pltpu.VMEM((frames, heads, 2 * tt, HD), BF16),
            pltpu.VMEM((frames, heads, 2 * tt, HD), BF16),
            pltpu.VMEM((frames, 8, HD), F32),
            pltpu.VMEM((frames, mps, 8, HD), F32),
            pltpu.VMEM((gain_rows, HD), F32),
            pltpu.VMEM((clips, frames, gain_rows, HD), F32),
            dma((frames, parts)),
            dma((frames, parts)),
            dma((frames, mps)),
            dma((frames, mps)),
            dma((frames, parts)),
            dma((frames, parts)),
            dma((frames, mps)),
            dma((frames, mps)),
            dma((clips, frames)),
            dma((clips, frames)),
            dma((5,)),
        ],
        compiler_params=pltpu.CompilerParams(
            collective_id=0, has_side_effects=True, vmem_limit_bytes=56 * 2**20
        ),
    )(
        query.reshape(count, width),
        key.reshape(count, width),
        value.reshape(count, width),
        gains,
        warp_lists.reshape(tiles),
        cotangent.reshape(frames * tt, width),
    )
    outs = pl.pallas_call(
        write_out,
        out_shape=tuple(jax.ShapeDtypeStruct(shape, kind) for shape, kind in results),
        in_specs=[vmem] * 5,
        out_specs=(pl.BlockSpec(memory_space=pl.ANY),) * 5,
        scratch_shapes=[dma((5,))],
    )(*(pltpu.with_memory_space_constraint(out, pltpu.VMEM) for out in outs))
    temporal, back_q, back_k, back_v, grad_gains = outs
    return (
        temporal.reshape(cotangent.shape),
        back_q.reshape(query.shape),
        back_k.reshape(query.shape),
        back_v.reshape(query.shape),
        grad_gains,
    )


def solution(mesh):
    sizes = (mesh.shape["clip"], mesh.shape["frame"], mesh.shape["mp"])
    return jax.shard_map(
        functools.partial(body, sizes),
        mesh=mesh,
        in_specs=(
            P("clip", "frame", None, None, "mp"),
            P("clip", "frame", None, None, "mp"),
            P("clip", "frame", None, None, "mp"),
            P(None, "mp"),
            P("clip", "frame", None),
            P("clip", None, "frame", None, "mp"),
        ),
        out_specs=(
            P("clip", None, "frame", None, "mp"),
            P("clip", "frame", None, None, "mp"),
            P("clip", "frame", None, None, "mp"),
            P("clip", "frame", None, None, "mp"),
            P(None, "mp"),
        ),
        check_vma=False,
    )
```
